128 devices in a mesh: rows: 2 (over core), cols: 64 (over z, y, x).
Axes of the slice: x: 4, y: 4, z: 4, core: 2. Of those that a mesh axis runs over, the one named last changes fastest.
Arguments:
- row_geom: float32 [3072, 8, 1024], P('cols', None, 'rows'), may hold values from -1 to 1
- col_geom: float32 [3072, 8, 1024], P('cols', None, 'rows'), may hold values from -1 to 1
- row_start: int32 [3072], P('cols'), may hold values from 1024 to 397951
- col_start: int32 [3072], P('cols'), may hold values from 512 to 398463, as said below
- block_count: int32 [64], P('cols'), may hold values from 1 to 48, 768 in all
- sketch: float32 [1024, 64], replicated, may hold values from -0.75 to 0.75
Outputs:
- left_factor: float32 [3072, 64, 1024], P('cols', None, 'rows')
- right_factor: float32 [3072, 64, 1024], P('cols', None, 'rows')
The draws below stay inside these ranges and needn't reach their ends.
Inputs may be any that keep to these rules, and one draw needn't show every extreme that they name: `block_count`: each owner's counts are at most 48; all counts together sum to exactly 48 // 4 times the number of owners. Places beyond an owner's count are unused. col_start minus row_start lies between -512 and 512.
All inputs are finite; a program needn't handle non-finite values. No bound on the sum of `block_count` on one device may be relied on, other than what follows from the above.
Results may differ from the reference program's by a relative error of at most 0.0003.
Values sent between devices are 32-bit elements; how exact they have to be, the bound alone decides.
A program may use at most 128 MiB of HBM per device.

```python
import math
import jax
import jax.numpy as jnp
import numpy as np
from jax import lax

BLK = 1024
RANK = 64
GEO = 8
PANELS = 400000
OWN = 48
BLOCKS = 3072
N_COLS = 64


def start_pair(key):
    anchor = jax.random.randint(jax.random.fold_in(key, 11), (BLOCKS,), BLK, PANELS - 2 * BLK, dtype=jnp.int32)
    offset = jax.random.randint(jax.random.fold_in(key, 12), (BLOCKS,), -(BLK // 2), BLK // 2 + 1, dtype=jnp.int32)
    return (anchor, anchor + offset)


def draw_row_start(key, part):
    return start_pair(key)[0]


def draw_col_start(key, part):
    return start_pair(key)[1]


def level_of(stream_key, shape, pieces, low, largest):
    gain = 1.0
    for position, shards_of in pieces:
        draws = jax.random.uniform(jax.random.fold_in(jax.random.fold_in(stream_key, 6), position), (shards_of,), jnp.float32, low / len(pieces), largest / len(pieces))
        gain = gain * jnp.repeat(jnp.exp(draws), shape[position] // shards_of).reshape((-1,) + (1,) * (len(shape) - 1 - position))
    return gain


def length_profile(amount, total, reach, slope):
    portions = [(1 << 20) // math.isqrt(standing ** slope) + 1 for standing in range(2, amount + 1)]
    surplus, given = total - reach - (amount - 1), [1] * (amount - 1)
    while surplus > 0:
        candidates = [i for i in range(amount - 1) if given[i] < reach]
        mass, left = sum([portions[i] for i in candidates]), surplus
        for i in candidates:
            more = min(reach - given[i], max(1, left * portions[i] // mass), surplus)
            given[i] = given[i] + more
            surplus = surplus - more
    return np.array([reach] + given)


def uneven_parts(key, number_of, total, bound, slope):
    if number_of == 2:
        one = jax.random.randint(key, (), max(1, total - bound), min(bound, total - 1) + 1)
        return jnp.stack([one, total - one])
    tallies = jnp.asarray(length_profile(number_of, total, bound, slope), jnp.int32)
    pairs = (number_of - 1) // 2
    donor, receiver = tallies[1:1 + 2 * pairs:2], tallies[2:2 + 2 * pairs:2]
    margin = jnp.minimum(donor - 1, bound - receiver)
    shifted = jax.random.randint(jax.random.fold_in(key, 1), (pairs,), 0, 1 << 20) % (margin + 1)
    tallies = tallies.at[1:1 + 2 * pairs:2].set(donor - shifted).at[2:2 + 2 * pairs:2].set(receiver + shifted)
    return tallies[jax.random.permutation(jax.random.fold_in(key, 2), number_of)]


def centred(own_key, dims, spread, limit, held_as=jnp.bfloat16):
    result = spread * jax.random.normal(own_key, dims, jnp.float32)
    return jnp.clip(result, min=-limit, max=limit).astype(held_as)


def setup_inputs(seed: int = 0) -> dict:
    streams_of = jax.random.split(jax.random.key(seed), 7)
    row_geom = jnp.clip(jax.random.uniform(streams_of[0], (BLOCKS, GEO, BLK), jnp.float32, -1.0, 1.0) * level_of(streams_of[0], (BLOCKS, GEO, BLK), ((0, 64), (2, 2)), -0.4, 0.0), -1.0, 1.0)
    col_geom = jnp.clip(jax.random.uniform(streams_of[1], (BLOCKS, GEO, BLK), jnp.float32, -1.0, 1.0) * level_of(streams_of[1], (BLOCKS, GEO, BLK), ((0, 64), (2, 2)), -0.4, 0.0), -1.0, 1.0)
    row_start = draw_row_start(jax.random.fold_in(streams_of[6], 71), 0)
    col_start = draw_col_start(jax.random.fold_in(streams_of[6], 71), 0)
    block_count = uneven_parts(streams_of[4], N_COLS, OWN // 4 * N_COLS, OWN, 2).astype(jnp.int32)
    sketch = centred(streams_of[5], (BLK, RANK), RANK ** -0.5, 0.75, jnp.float32)
    return dict(row_geom=row_geom, col_geom=col_geom, row_start=row_start, col_start=col_start, block_count=block_count, sketch=sketch)


HIGHEST = lax.Precision.HIGHEST

def kernel_block(row_geo, col_geo, start_row, start_col, offset):
    sep_x = row_geo[:, 0, :, None] - col_geo[:, 0, None, :]
    sep_y = row_geo[:, 1, :, None] - col_geo[:, 1, None, :]
    sep_z = row_geo[:, 2, :, None] - col_geo[:, 2, None, :]
    row_area = 0.1 + 0.05 * row_geo[:, 6, :, None]
    col_area = 0.1 + 0.05 * col_geo[:, 6, None, :]
    inverse = 1.0 / (sep_x * sep_x + sep_y * sep_y + sep_z * sep_z + row_area + col_area)
    normal_dot = row_geo[:, 3, :, None] * col_geo[:, 3, None, :] + row_geo[:, 4, :, None] * col_geo[:, 4, None, :] + row_geo[:, 5, :, None] * col_geo[:, 5, None, :]
    row_proj = row_geo[:, 3, :, None] * sep_x + row_geo[:, 4, :, None] * sep_y + row_geo[:, 5, :, None] * sep_z
    col_proj = col_geo[:, 3, None, :] * sep_x + col_geo[:, 4, None, :] * sep_y + col_geo[:, 5, None, :] * sep_z
    influence = col_area * (normal_dot - 3.0 * row_proj * col_proj * inverse) * inverse * jnp.sqrt(inverse)
    self_term = 4.0 + 2.0 * row_geo[:, 7, :, None]
    row_ids = offset + jnp.arange(row_geo.shape[2], dtype=jnp.int32)[:, None]
    col_ids = jnp.arange(col_geo.shape[2], dtype=jnp.int32)[None, :]
    distance = (start_row - start_col).astype(jnp.int32)[:, None, None]
    match = (col_ids - row_ids)[None, :, :] == distance
    return jnp.where(match, self_term, influence)

def factor_pair(gram, projected):
    rank = gram.shape[1]
    trace = jnp.trace(gram, axis1=1, axis2=2)
    ridge = 0.01 * trace / rank + 0.001
    system = gram + ridge[:, None, None] * jnp.eye(rank, dtype=gram.dtype)[None]
    lower = jnp.linalg.cholesky(system)
    half = lax.linalg.triangular_solve(lower, projected, left_side=True, lower=True)
    return lax.linalg.triangular_solve(lower, half, left_side=True, lower=True, transpose_a=True)

def reference(row_geom, col_geom, row_start, col_start, block_count, sketch):
    blocks = row_geom.shape[0]
    owned = blocks // block_count.shape[0]
    live = jnp.arange(blocks, dtype=jnp.int32) % owned < jnp.repeat(block_count, owned)

    def one_block(packed):
        row_geo, col_geo, first_row, first_col, is_live = packed
        block = kernel_block(row_geo[None], col_geo[None], first_row[None], first_col[None], jnp.int32(0))
        sketched = jnp.einsum('gik,kr->gir', block, sketch, precision=HIGHEST)
        gram = jnp.einsum('gir,gis->grs', sketched, sketched, precision=HIGHEST)
        projected = jnp.einsum('gik,gir->grk', block, sketched, precision=HIGHEST)
        right = factor_pair(gram, projected)
        left = jnp.transpose(sketched, (0, 2, 1))
        return (jnp.where(is_live, left[0], 0.0), jnp.where(is_live, right[0], 0.0))
    return lax.map(one_block, (row_geom, col_geom, row_start, col_start, live))
```

```python
import functools

import jax
import jax.numpy as jnp
from jax import lax
from jax.experimental import pallas as pl
from jax.experimental.pallas import tpu as pltpu
from jax.sharding import PartitionSpec as P

F32, BF16 = jnp.float32, jnp.bfloat16
GROUP = 8
STRIPE = 256
CHUNK = 128
MESH = pl.DeviceIdType.MESH
ROW_ORDER, COL_ORDER = (0, 0, 1, 1, 0, 2), (0, 1, 0, 1, 2, 0)


def nn(a, b):
    return jnp.dot(a, b, preferred_element_type=F32)


def nt(a, b):
    return lax.dot_general(a, b, (((1,), (1,)), ((), ())), preferred_element_type=F32)


def pieces(x):
    high = x.astype(BF16).astype(F32)
    rest = x - high
    middle = rest.astype(BF16).astype(F32)
    return high, middle, rest - middle


def stacked(x, order):
    parts = pieces(x)
    return jnp.concatenate([parts[k] for k in order], 0).astype(BF16)


def halves(x):
    high = x.astype(BF16)
    return high, (x - high.astype(F32)).astype(BF16)


def row_features(g):
    sub = lax.broadcasted_iota(jnp.int32, g.shape, 0)
    x = [g[k : k + 1] for k in range(3)]
    n = [g[k : k + 1] for k in range(3, 6)]
    p = n[0] * x[0] + n[1] * x[1] + n[2] * x[2]
    sq = x[0] * x[0] + x[1] * x[1] + x[2] * x[2] + (0.1 + 0.05 * g[6:7])
    base = jnp.where(sub < 6, g, jnp.where(sub == 6, 1.0, sq))
    mid = (sub >= 3) & (sub < 6)
    last = base * jnp.where(mid, sq, p)
    return base, jnp.concatenate([base, base * x[0], base * x[1], base * x[2], last], 0)


def col_features(c):
    sub = lax.broadcasted_iota(jnp.int32, c.shape, 0)
    y = [c[k : k + 1] for k in range(3)]
    m = [c[k : k + 1] for k in range(3, 6)]
    q = m[0] * y[0] + m[1] * y[1] + m[2] * y[2]
    area = 0.1 + 0.05 * c[6:7]
    sq = y[0] * y[0] + y[1] * y[1] + y[2] * y[2] + area
    w = -3.0 * area
    mid = (sub >= 3) & (sub < 6)
    up = jnp.where(mid, pltpu.roll(c, 3, 0), 0.0)
    own = jnp.where(mid, area * c, 0.0)
    down = pltpu.roll(c, 5, 0)
    dist = jnp.where(
        sub < 3, -2.0 * c, jnp.where(sub == 6, sq, jnp.where(sub == 7, 1.0, 0.0))
    )
    numer = jnp.concatenate(
        [up * (w * q) + own * sq]
        + [up * (-w * m[b]) - 2.0 * y[b] * own for b in range(3)]
        + [jnp.where(sub < 3, w * down, jnp.where(sub == 6, -w * q, own))],
        0,
    )
    return dist, numer


def block_factors(g, c, delta, live, sk_ref, y_ref, z_ref, fd, fw, ru, rw, bh, bl):
    width, rank = g.shape[1], y_ref.shape[0]
    base, wide = row_features(g)
    ru[...] = stacked(base, ROW_ORDER)
    rw[...] = stacked(wide, ROW_ORDER)
    dist, numer = col_features(c)
    fd[...] = stacked(dist, COL_ORDER).T
    fw[...] = stacked(numer, COL_ORDER).T
    gap = lax.broadcasted_iota(jnp.int32, (CHUNK, STRIPE), 0) - lax.broadcasted_iota(
        jnp.int32, (CHUNK, STRIPE), 1
    )

    def project(prev):
        s, pair, high = prev
        both = nt(pair, bh[s % 2])
        z = both[:rank] + both[rank:] + nt(high, bl[s % 2])
        z_ref[...] = z if s == 0 else z_ref[...] + z

    prev = None
    for s in range(width // STRIPE):
        cols = slice(s * STRIPE, (s + 1) * STRIPE)
        u, w = ru[:, cols], rw[:, cols]
        own = 4.0 + 2.0 * g[7:8, cols]
        for j in range(0, width, CHUNK):
            d = nn(fd[j : j + CHUNK, :], u)
            h = nn(fw[j : j + CHUNK, :], w)
            t = lax.rsqrt(d)
            t2 = t * t
            a = (h * t) * (t2 * t2)
            a = jnp.where(gap == delta + (s * STRIPE - j), own, a)
            high, low = halves(a)
            bh[s % 2, j : j + CHUNK, :] = high
            bl[s % 2, j : j + CHUNK, :] = low
        if prev is not None:
            project(prev)
        both = nn(sk_ref[...], bh[s % 2])
        y = (both[:rank] + both[rank:] + nn(sk_ref[:rank, :], bl[s % 2])) * live
        y_ref[:, cols] = y
        high, low = halves(y)
        prev = (s, jnp.concatenate([high, low], 0), high)
    project(prev)


def system_of(y):
    rank = y.shape[0]
    high, low = halves(y)
    both = nt(jnp.concatenate([high, low], 0), high)
    cross = both[rank:]
    gram = both[:rank] + (cross + cross.T)
    one = (
        lax.broadcasted_iota(jnp.int32, (rank, rank), 0)
        == lax.broadcasted_iota(jnp.int32, (rank, rank), 1)
    ).astype(F32)
    diagonal = jnp.sum(gram * one, axis=0, keepdims=True)
    trace = jnp.sum(diagonal, axis=1, keepdims=True)
    lam = 0.01 * trace / rank + 0.001
    return jnp.concatenate([one, gram + lam * one], 1)


def eliminated(a):
    rank = a.shape[1]
    sub = lax.broadcasted_iota(jnp.int32, (1, rank, 1), 1)
    for k in range(rank):
        row = a[:, k : k + 1, :] * (1.0 / a[:, k : k + 1, rank + k : rank + k + 1])
        a = jnp.where(sub == k, row, a - a[:, :, rank + k : rank + k + 1] * row)
    return a


def times(inverse, z):
    ih, im, il = pieces(inverse)
    zh, zm, zl = pieces(z)
    left = jnp.concatenate([ih, im, ih, im, il, ih], 1).astype(BF16)
    right = jnp.concatenate([zh, zh, zm, zm, zh, zl], 0).astype(BF16)
    return nn(left, right)


def kernel(
    rs_ref, cs_ref, count_ref, row_ref, col_ref, sketch_ref, left_ref, right_ref,
    geo, sk_ref, ybuf, zbuf, mats, fd, fw, ru, rw, bh, bl,
    geo_local, geo_send, geo_recv, out_local, out_send, out_recv,
):
    share, rank, width = ybuf.shape
    half = width // 2
    me = lax.axis_index("rows")
    other = 1 - me

    barrier = pltpu.get_barrier_semaphore()
    pl.semaphore_signal(barrier, inc=1, device_id={"rows": other}, device_id_type=MESH)
    pl.semaphore_wait(barrier, 1)

    mine = pl.ds(pl.multiple_of(me * half, half), half)
    theirs = pl.ds(pl.multiple_of(other * half, half), half)
    moves = []
    for k, ref in enumerate((row_ref, col_ref)):
        moves.append(
            pltpu.make_async_remote_copy(
                src_ref=ref.at[pl.ds(other * share, share)],
                dst_ref=geo.at[k, :, :, mine],
                send_sem=geo_send.at[k],
                recv_sem=geo_recv.at[k],
                device_id={"rows": other},
                device_id_type=MESH,
            )
        )
        moves.append(
            pltpu.make_async_copy(
                ref.at[pl.ds(me * share, share)], geo.at[k, :, :, mine], geo_local.at[k]
            )
        )
    for move in moves:
        move.start()

    s = sketch_ref[...]
    high = s.astype(BF16).astype(F32)
    sk_ref[...] = jnp.concatenate([high, s - high], 1).T.astype(BF16)
    for move in moves:
        move.wait()

    def outgoing(which, buf, out, g):
        blocks = pl.ds(g * GROUP, GROUP)
        places = pl.ds(me * share + g * GROUP, GROUP)
        here = pltpu.make_async_copy(
            buf.at[blocks, :, mine], out.at[places], out_local.at[which, g]
        )
        there = pltpu.make_async_remote_copy(
            src_ref=buf.at[blocks, :, theirs],
            dst_ref=out.at[places],
            send_sem=out_send.at[which, g],
            recv_sem=out_recv.at[which, g],
            device_id={"rows": other},
            device_id_type=MESH,
        )
        return here, there

    def group_step(g, carry):
        def block_step(b, carry):
            k = g * GROUP + b
            place = me * share + k
            delta = rs_ref[place] - cs_ref[place]
            live = jnp.where(place < count_ref[0], 1.0, 0.0)
            block_factors(
                geo[0, k], geo[1, k], delta, live, sk_ref, ybuf.at[k], zbuf.at[k],
                fd, fw, ru, rw, bh, bl,
            )
            mats[b] = system_of(ybuf[k])
            return carry

        lax.fori_loop(0, GROUP, block_step, 0)
        for move in outgoing(0, ybuf, left_ref, g):
            move.start()
        mats[...] = eliminated(mats[...])

        def solve_step(b, carry):
            k = g * GROUP + b
            zbuf[k] = times(mats[b][:, :rank], zbuf[k])
            return carry

        lax.fori_loop(0, GROUP, solve_step, 0)
        for move in outgoing(1, zbuf, right_ref, g):
            move.start()
        return carry

    groups = share // GROUP
    lax.fori_loop(0, groups, group_step, 0)
    for g in range(groups):
        for which, (buf, out) in enumerate(((ybuf, left_ref), (zbuf, right_ref))):
            for move in outgoing(which, buf, out, g):
                move.wait()


def on_device(row_geom, col_geom, row_start, col_start, block_count, sketch):
    owned, geo_count, half = row_geom.shape
    rank = sketch.shape[1]
    share, width = owned // 2, 2 * half
    groups = share // GROUP
    smem = pl.BlockSpec(memory_space=pltpu.SMEM)
    hbm = pl.BlockSpec(memory_space=pl.ANY)
    dma = pltpu.SemaphoreType.DMA
    return pl.pallas_call(
        kernel,
        out_shape=[jax.ShapeDtypeStruct((owned, rank, half), F32)] * 2,
        in_specs=[smem, smem, smem, hbm, hbm, pl.BlockSpec(memory_space=pltpu.VMEM)],
        out_specs=[hbm, hbm],
        scratch_shapes=[
            pltpu.VMEM((2, share, geo_count, width), F32),
            pltpu.VMEM((2 * rank, width), BF16),
            pltpu.VMEM((share, rank, width), F32),
            pltpu.VMEM((share, rank, width), F32),
            pltpu.VMEM((GROUP, rank, 2 * rank), F32),
            pltpu.VMEM((width, 48), BF16),
            pltpu.VMEM((width, 240), BF16),
            pltpu.VMEM((48, width), BF16),
            pltpu.VMEM((240, width), BF16),
            pltpu.VMEM((2, width, STRIPE), BF16),
            pltpu.VMEM((2, width, STRIPE), BF16),
            dma((2,)), dma((2,)), dma((2,)),
            dma((2, groups)), dma((2, groups)), dma((2, groups)),
        ],
        compiler_params=pltpu.CompilerParams(
            collective_id=0, has_side_effects=True, vmem_limit_bytes=48 << 20
        ),
    )(row_start, col_start, block_count, row_geom, col_geom, sketch)


def solution(mesh):
    placed = (
        P("cols", None, "rows"),
        P("cols", None, "rows"),
        P("cols"),
        P("cols"),
        P("cols"),
        P(),
    )
    return jax.shard_map(
        on_device,
        mesh=mesh,
        in_specs=placed,
        out_specs=(P("cols", None, "rows"), P("cols", None, "rows")),
        check_vma=False,
    )
```

```python
import functools

import jax
import jax.numpy as jnp
from jax import lax
from jax.experimental import pallas as pl
from jax.experimental.pallas import tpu as pltpu
from jax.sharding import PartitionSpec as P

F32, BF16 = jnp.float32, jnp.bfloat16
PIVOTS = 2
TOGETHER = 4
STRIPE = 512
CHUNK = 256
MESH = pl.DeviceIdType.MESH
ROW_ORDER, COL_ORDER = (0, 0, 1, 1, 0, 2), (0, 1, 0, 1, 2, 0)


def nn(a, b):
    return jnp.dot(a, b, preferred_element_type=F32)


def nt(a, b):
    return lax.dot_general(a, b, (((1,), (1,)), ((), ())), preferred_element_type=F32)


def pieces(x):
    high = x.astype(BF16).astype(F32)
    rest = x - high
    middle = rest.astype(BF16).astype(F32)
    return high, middle, rest - middle


def stacked(x, order):
    parts = pieces(x)
    return jnp.concatenate([parts[k] for k in order], 0).astype(BF16)


def halves(x):
    high = x.astype(BF16)
    return high, (x - high.astype(F32)).astype(BF16)


def row_features(g):
    sub = lax.broadcasted_iota(jnp.int32, g.shape, 0)
    x = [g[k : k + 1] for k in range(3)]
    n = [g[k : k + 1] for k in range(3, 6)]
    p = n[0] * x[0] + n[1] * x[1] + n[2] * x[2]
    sq = x[0] * x[0] + x[1] * x[1] + x[2] * x[2] + (0.1 + 0.05 * g[6:7])
    base = jnp.where(sub < 6, g, jnp.where(sub == 6, 1.0, sq))
    mid = (sub >= 3) & (sub < 6)
    last = base * jnp.where(mid, sq, p)
    return base, jnp.concatenate([base, base * x[0], base * x[1], base * x[2], last], 0)


def col_features(c):
    sub = lax.broadcasted_iota(jnp.int32, c.shape, 0)
    y = [c[k : k + 1] for k in range(3)]
    m = [c[k : k + 1] for k in range(3, 6)]
    q = m[0] * y[0] + m[1] * y[1] + m[2] * y[2]
    area = 0.1 + 0.05 * c[6:7]
    sq = y[0] * y[0] + y[1] * y[1] + y[2] * y[2] + area
    w = -3.0 * area
    mid = (sub >= 3) & (sub < 6)
    up = jnp.where(mid, pltpu.roll(c, 3, 0), 0.0)
    own = jnp.where(mid, area * c, 0.0)
    down = pltpu.roll(c, 5, 0)
    dist = jnp.where(
        sub < 3, -2.0 * c, jnp.where(sub == 6, sq, jnp.where(sub == 7, 1.0, 0.0))
    )
    numer = jnp.concatenate(
        [up * (w * q) + own * sq]
        + [up * (-w * m[b]) - 2.0 * y[b] * own for b in range(3)]
        + [jnp.where(sub < 3, w * down, jnp.where(sub == 6, -w * q, own))],
        0,
    )
    return dist, numer


def put_features(g, c, fd, fw, ru, rw):
    base, wide = row_features(g)
    ru[...] = stacked(base, ROW_ORDER)
    rw[...] = stacked(wide, ROW_ORDER)
    dist, numer = col_features(c)
    fd[...] = stacked(dist, COL_ORDER).T
    fw[...] = stacked(numer, COL_ORDER).T


def identity(rank):
    return (
        lax.broadcasted_iota(jnp.int32, (rank, rank), 0)
        == lax.broadcasted_iota(jnp.int32, (rank, rank), 1)
    ).astype(F32)


def system_of(products):
    rank = products.shape[1]
    cross = products[rank:]
    gram = products[:rank] + (cross + cross.T)
    one = identity(rank)
    diagonal = jnp.sum(gram * one, axis=0, keepdims=True)
    lam = 0.01 * jnp.sum(diagonal, axis=1, keepdims=True) / rank + 0.001
    return jnp.concatenate([one, gram + lam * one], 1)


def eliminated(a, first, last):
    rank = a.shape[0]
    sub = lax.broadcasted_iota(jnp.int32, (rank, 1), 0)
    for k in range(first, last):
        column = jnp.broadcast_to(a[:, rank + k : rank + k + 1], a.shape)
        row = a[k : k + 1, :] / column[k : k + 1, :]
        a = jnp.where(sub == k, row, a - column * row)
    return a


def times(inverse, z):
    ih, il = halves(inverse)
    zh, zl = halves(z)
    left = jnp.concatenate([inverse_piece.astype(F32) for inverse_piece in (ih, il, ih, il)], 1)
    return nn(left.astype(BF16), jnp.concatenate([zh, zh, zl, zl], 0))


def blocks_step(geo, k, deltas, lives, sk_ref, ybuf, rbuf, zprev, sys_ref, fd, fw, ru, rw, bh, bl):
    rank, width = zprev.shape[1:]
    gap = lax.broadcasted_iota(jnp.int32, (CHUNK, STRIPE), 0) - lax.broadcasted_iota(
        jnp.int32, (CHUNK, STRIPE), 1
    )
    systems = [sys_ref[t] for t in range(TOGETHER)]
    done = 0

    def project(prev):
        slot, pair, high = prev
        both = nt(pair, bh[slot])
        return both[:rank] + both[rank:] + nt(high, bl[slot])

    stripes = width // STRIPE
    finished = []
    for t in range(TOGETHER):
        prev = z = products = None
        for s in range(stripes):
            slot = s % 2
            cols = slice(s * STRIPE, (s + 1) * STRIPE)
            u, w = ru[:, cols], rw[:, cols]
            own = 4.0 + 2.0 * geo[k + t, 0, 7:8, cols]
            for j in range(0, width, CHUNK):
                d = nn(fd[j : j + CHUNK, :], u)
                h = nn(fw[j : j + CHUNK, :], w)
                r = lax.rsqrt(d)
                r2 = r * r
                a = (h * r) * (r2 * r2)
                a = jnp.where(gap == deltas[t] + (s * STRIPE - j), own, a)
                high, low = halves(a)
                bh[slot, j : j + CHUNK, :] = high
                bl[slot, j : j + CHUNK, :] = low
                upto = min(rank, done + PIVOTS)
                systems = [eliminated(a, done, upto) for a in systems]
                done = upto
            if prev is not None:
                part = project(prev)
                z = part if z is None else z + part
            if s == stripes - 1:
                if t == TOGETHER - 1:
                    for b in range(TOGETHER):
                        rbuf[k + b] = times(systems[b][:, :rank], zprev[b])
                put_features(geo[k + t + 1, 0], geo[k + t + 1, 1], fd, fw, ru, rw)
            both = nn(sk_ref[...], bh[slot])
            y = (both[:rank] + both[rank:] + nn(sk_ref[:rank, :], bl[slot])) * lives[t]
            ybuf[k + t, :, cols] = y
            high, low = halves(y)
            pair = jnp.concatenate([high, low], 0)
            part = nt(pair, high)
            products = part if products is None else products + part
            prev = (slot, pair, high)
        finished.append((system_of(products), z + project(prev)))
    for t, (system, z) in enumerate(finished):
        sys_ref[t] = system
        zprev[t] = z


def kernel(
    rs_hbm, cs_hbm, count_hbm, row_ref, col_ref, sketch_ref, left_ref, right_ref,
    geo, sk_ref, ybuf, rbuf, zprev, sys_ref, fd, fw, ru, rw, bh, bl, rs_ref, cs_ref, count_ref,
    small_sem, geo_local, geo_send, geo_recv, out_local, out_send, out_recv,
):
    share, rank, width = ybuf.shape
    half = width // 2
    me = lax.axis_index("rows")
    other = 1 - me

    small = [
        pltpu.make_async_copy(src, dst, small_sem.at[k])
        for k, (src, dst) in enumerate(
            ((rs_hbm, rs_ref), (cs_hbm, cs_ref), (count_hbm, count_ref))
        )
    ]
    for move in small:
        move.start()
    barrier = pltpu.get_barrier_semaphore()
    pl.semaphore_signal(barrier, inc=1, device_id={"rows": other}, device_id_type=MESH)
    pl.semaphore_wait(barrier, 1)

    mine = pl.ds(pl.multiple_of(me * half, half), half)
    theirs = pl.ds(pl.multiple_of(other * half, half), half)
    moves = []
    for k, ref in enumerate((row_ref, col_ref)):
        moves.append(
            pltpu.make_async_remote_copy(
                src_ref=ref.at[pl.ds(other * share, share)],
                dst_ref=geo.at[pl.ds(0, share), k, :, mine],
                send_sem=geo_send.at[k],
                recv_sem=geo_recv.at[k],
                device_id={"rows": other},
                device_id_type=MESH,
            )
        )
        moves.append(
            pltpu.make_async_copy(
                ref.at[pl.ds(me * share, share)],
                geo.at[pl.ds(0, share), k, :, mine],
                geo_local.at[k],
            )
        )
    for move in moves:
        move.start()

    s = sketch_ref[...]
    high = s.astype(BF16).astype(F32)
    sk_ref[...] = jnp.concatenate([high, s - high], 0).astype(BF16)
    for t in range(TOGETHER):
        sys_ref[t] = jnp.concatenate([identity(rank)] * 2, 1)
    zprev[...] = jnp.zeros_like(zprev)
    geo[share] = jnp.zeros(geo.shape[1:], F32)
    for move in small + moves:
        move.wait()
    put_features(geo[0, 0], geo[0, 1], fd, fw, ru, rw)

    def outgoing(which, first, count):
        buf, out, shift = ((ybuf, left_ref, 0), (rbuf, right_ref, TOGETHER))[which]
        blocks = pl.ds(first + shift, count)
        places = pl.ds(me * share + first, count)
        here = pltpu.make_async_copy(
            buf.at[blocks, :, mine], out.at[places], out_local.at[which]
        )
        there = pltpu.make_async_remote_copy(
            src_ref=buf.at[blocks, :, theirs],
            dst_ref=out.at[places],
            send_sem=out_send.at[which],
            recv_sem=out_recv.at[which],
            device_id={"rows": other},
            device_id_type=MESH,
        )
        return here, there

    def step(m, carry):
        k = TOGETHER * m
        places = [me * share + k + t for t in range(TOGETHER)]
        deltas = [rs_ref[p] - cs_ref[p] for p in places]
        lives = [jnp.where(p < count_ref[0], 1.0, 0.0) for p in places]
        blocks_step(
            geo, k, deltas, lives, sk_ref, ybuf, rbuf, zprev, sys_ref, fd, fw, ru, rw, bh, bl
        )
        for move in outgoing(0, k, TOGETHER):
            move.start()

        @pl.when(m > 0)
        def _():
            for move in outgoing(1, k - TOGETHER, TOGETHER):
                move.start()

        return carry

    lax.fori_loop(0, share // TOGETHER, step, 0)
    systems = [eliminated(sys_ref[t], 0, rank) for t in range(TOGETHER)]
    for t in range(TOGETHER):
        rbuf[share + t] = times(systems[t][:, :rank], zprev[t])
    for move in outgoing(1, share - TOGETHER, TOGETHER):
        move.start()
    for which in range(2):
        for move in outgoing(which, 0, share):
            move.wait()


def on_device(row_geom, col_geom, row_start, col_start, block_count, sketch):
    owned, geo_count, half = row_geom.shape
    rank = sketch.shape[1]
    share, width = owned // 2, 2 * half
    hbm = pl.BlockSpec(memory_space=pl.ANY)
    dma = pltpu.SemaphoreType.DMA
    return pl.pallas_call(
        kernel,
        out_shape=[jax.ShapeDtypeStruct((owned, rank, half), F32)] * 2,
        in_specs=[hbm] * 5 + [pl.BlockSpec(memory_space=pltpu.VMEM)],
        out_specs=[hbm, hbm],
        scratch_shapes=[
            pltpu.VMEM((share + 1, 2, geo_count, width), F32),
            pltpu.VMEM((2 * rank, width), BF16),
            pltpu.VMEM((share, rank, width), F32),
            pltpu.VMEM((share + TOGETHER, rank, width), F32),
            pltpu.VMEM((TOGETHER, rank, width), F32),
            pltpu.VMEM((TOGETHER, rank, 2 * rank), F32),
            pltpu.VMEM((width, 48), BF16),
            pltpu.VMEM((width, 240), BF16),
            pltpu.VMEM((48, width), BF16),
            pltpu.VMEM((240, width), BF16),
            pltpu.VMEM((2, width, STRIPE), BF16),
            pltpu.VMEM((2, width, STRIPE), BF16),
            pltpu.SMEM(row_start.shape, jnp.int32),
            pltpu.SMEM(col_start.shape, jnp.int32),
            pltpu.SMEM(block_count.shape, jnp.int32),
            dma((3,)), dma((2,)), dma((2,)), dma((2,)), dma((2,)), dma((2,)), dma((2,)),
        ],
        compiler_params=pltpu.CompilerParams(
            collective_id=0, has_side_effects=True, vmem_limit_bytes=48 << 20
        ),
    )(row_start, col_start, block_count, row_geom, col_geom, sketch.T)


def solution(mesh):
    placed = (
        P("cols", None, "rows"),
        P("cols", None, "rows"),
        P("cols"),
        P("cols"),
        P("cols"),
        P(),
    )
    return jax.shard_map(
        on_device,
        mesh=mesh,
        in_specs=placed,
        out_specs=(P("cols", None, "rows"), P("cols", None, "rows")),
        check_vma=False,
    )
```

```python
import functools

import jax
import jax.numpy as jnp
from jax import lax
from jax.experimental import pallas as pl
from jax.experimental.pallas import tpu as pltpu
from jax.sharding import PartitionSpec as P

F32, BF16 = jnp.float32, jnp.bfloat16
PIVOTS = 3
TOGETHER = 4
STRIPE = 512
CHUNK = 256
MESH = pl.DeviceIdType.MESH
ROW_ORDER, COL_ORDER = (0, 0, 1, 1, 0, 2), (0, 1, 0, 1, 2, 0)


def nn(a, b):
    return jnp.dot(a, b, preferred_element_type=F32)


def nt(a, b):
    return lax.dot_general(a, b, (((1,), (1,)), ((), ())), preferred_element_type=F32)


def pieces(x):
    high = x.astype(BF16).astype(F32)
    rest = x - high
    middle = rest.astype(BF16).astype(F32)
    return high, middle, rest - middle


def stacked(x, order):
    parts = pieces(x)
    return jnp.concatenate([parts[k] for k in order], 0).astype(BF16)


def halves(x):
    high = x.astype(BF16)
    return high, (x - high.astype(F32)).astype(BF16)


def row_features(g):
    sub = lax.broadcasted_iota(jnp.int32, g.shape, 0)
    x = [g[k : k + 1] for k in range(3)]
    n = [g[k : k + 1] for k in range(3, 6)]
    p = n[0] * x[0] + n[1] * x[1] + n[2] * x[2]
    sq = x[0] * x[0] + x[1] * x[1] + x[2] * x[2] + (0.1 + 0.05 * g[6:7])
    base = jnp.where(sub < 6, g, jnp.where(sub == 6, 1.0, sq))
    mid = (sub >= 3) & (sub < 6)
    last = base * jnp.where(mid, sq, p)
    return base, jnp.concatenate([base, base * x[0], base * x[1], base * x[2], last], 0)


def col_features(c):
    sub = lax.broadcasted_iota(jnp.int32, c.shape, 0)
    y = [c[k : k + 1] for k in range(3)]
    m = [c[k : k + 1] for k in range(3, 6)]
    q = m[0] * y[0] + m[1] * y[1] + m[2] * y[2]
    area = 0.1 + 0.05 * c[6:7]
    sq = y[0] * y[0] + y[1] * y[1] + y[2] * y[2] + area
    w = -3.0 * area
    mid = (sub >= 3) & (sub < 6)
    up = jnp.where(mid, pltpu.roll(c, 3, 0), 0.0)
    own = jnp.where(mid, area * c, 0.0)
    down = pltpu.roll(c, 5, 0)
    dist = jnp.where(
        sub < 3, -2.0 * c, jnp.where(sub == 6, sq, jnp.where(sub == 7, 1.0, 0.0))
    )
    numer = jnp.concatenate(
        [up * (w * q) + own * sq]
        + [up * (-w * m[b]) - 2.0 * y[b] * own for b in range(3)]
        + [jnp.where(sub < 3, w * down, jnp.where(sub == 6, -w * q, own))],
        0,
    )
    return dist, numer


def put_features(g, c, fd, fw, ru, rw):
    base, wide = row_features(g)
    ru[...] = stacked(base, ROW_ORDER)
    rw[...] = stacked(wide, ROW_ORDER)
    dist, numer = col_features(c)
    fd[...] = stacked(dist, COL_ORDER).T
    fw[...] = stacked(numer, COL_ORDER).T


def identity(rank):
    return (
        lax.broadcasted_iota(jnp.int32, (rank, rank), 0)
        == lax.broadcasted_iota(jnp.int32, (rank, rank), 1)
    ).astype(F32)


def system_of(products):
    rank = products.shape[1]
    cross = products[rank:]
    gram = products[:rank] + (cross + cross.T)
    one = identity(rank)
    diagonal = jnp.sum(gram * one, axis=0, keepdims=True)
    lam = 0.01 * jnp.sum(diagonal, axis=1, keepdims=True) / rank + 0.001
    return jnp.concatenate([one, gram + lam * one], 1)


def eliminated(a, first, last):
    rank = a.shape[0]
    sub = lax.broadcasted_iota(jnp.int32, (rank, 1), 0)
    for k in range(first, last):
        column = jnp.broadcast_to(a[:, rank + k : rank + k + 1], a.shape)
        row = a[k : k + 1, :] / column[k : k + 1, :]
        a = jnp.where(sub == k, row, a - column * row)
    return a


def times(inverse, z):
    ih, il = halves(inverse)
    zh, zl = halves(z)
    left = jnp.concatenate([inverse_piece.astype(F32) for inverse_piece in (ih, il, ih, il)], 1)
    return nn(left.astype(BF16), jnp.concatenate([zh, zh, zl, zl], 0))


def blocks_step(geo, k, deltas, lives, sk_ref, ybuf, rbuf, zprev, sys_ref, fd, fw, ru, rw, bh, bl):
    rank, width = zprev.shape[1:]
    gap = lax.broadcasted_iota(jnp.int32, (CHUNK, STRIPE), 0) - lax.broadcasted_iota(
        jnp.int32, (CHUNK, STRIPE), 1
    )
    systems = [sys_ref[t] for t in range(TOGETHER)]
    done = 0

    def project(prev):
        slot, pair, high = prev
        both = nt(pair, bh[slot])
        return both[:rank] + both[rank:] + nt(high, bl[slot])

    stripes = width // STRIPE
    zs, grams = [None] * TOGETHER, [None] * TOGETHER
    prev = None

    def add_projection():
        t, part = prev[0], project(prev[1:])
        zs[t] = part if zs[t] is None else zs[t] + part

    for t in range(TOGETHER):
        for s in range(stripes):
            slot = (t * stripes + s) % 2
            cols = slice(s * STRIPE, (s + 1) * STRIPE)
            u, w = ru[:, cols], rw[:, cols]
            own = 4.0 + 2.0 * geo[k + t, 0, 7:8, cols]
            for j in range(0, width, CHUNK):
                d = nn(fd[j : j + CHUNK, :], u)
                h = nn(fw[j : j + CHUNK, :], w)
                r = lax.rsqrt(d)
                r2 = r * r
                a = (h * r) * (r2 * r2)
                a = jnp.where(gap == deltas[t] + (s * STRIPE - j), own, a)
                high, low = halves(a)
                bh[slot, j : j + CHUNK, :] = high
                bl[slot, j : j + CHUNK, :] = low
                upto = min(rank, done + PIVOTS)
                systems = [eliminated(m, done, upto) for m in systems]
                done = upto
            if prev is not None:
                add_projection()
            if s == stripes - 1:
                if t == TOGETHER - 1:
                    for b in range(TOGETHER):
                        rbuf[k + b] = times(systems[b][:, :rank], zprev[b])
                put_features(geo[k + t + 1, 0], geo[k + t + 1, 1], fd, fw, ru, rw)
            both = nn(sk_ref[...], bh[slot])
            y = (both[:rank] + both[rank:] + nn(sk_ref[:rank, :], bl[slot])) * lives[t]
            ybuf[k + t, :, cols] = y
            high, low = halves(y)
            pair = jnp.concatenate([high, low], 0)
            part = nt(pair, high)
            grams[t] = part if grams[t] is None else grams[t] + part
            prev = (t, slot, pair, high)
    add_projection()
    for t in range(TOGETHER):
        sys_ref[t] = system_of(grams[t])
        zprev[t] = zs[t]


def kernel(
    rs_hbm, cs_hbm, count_hbm, row_ref, col_ref, sketch_ref, left_ref, right_ref,
    geo, sk_ref, ybuf, rbuf, zprev, sys_ref, fd, fw, ru, rw, bh, bl, rs_ref, cs_ref, count_ref,
    small_sem, geo_local, geo_send, geo_recv, out_local, out_send, out_recv,
):
    share, rank, width = ybuf.shape
    half = width // 2
    me = lax.axis_index("rows")
    other = 1 - me

    small = [
        pltpu.make_async_copy(src, dst, small_sem.at[k])
        for k, (src, dst) in enumerate(
            ((rs_hbm, rs_ref), (cs_hbm, cs_ref), (count_hbm, count_ref))
        )
    ]
    for move in small:
        move.start()
    barrier = pltpu.get_barrier_semaphore()
    pl.semaphore_signal(barrier, inc=1, device_id={"rows": other}, device_id_type=MESH)
    pl.semaphore_wait(barrier, 1)

    mine = pl.ds(pl.multiple_of(me * half, half), half)
    theirs = pl.ds(pl.multiple_of(other * half, half), half)
    def incoming(part, first, count):
        moves = []
        for k, ref in enumerate((row_ref, col_ref)):
            into = geo.at[pl.ds(first, count), k, :, mine]
            moves.append(
                pltpu.make_async_remote_copy(
                    src_ref=ref.at[pl.ds(other * share + first, count)],
                    dst_ref=into,
                    send_sem=geo_send.at[part, k],
                    recv_sem=geo_recv.at[part, k],
                    device_id={"rows": other},
                    device_id_type=MESH,
                )
            )
            moves.append(
                pltpu.make_async_copy(
                    ref.at[pl.ds(me * share + first, count)], into, geo_local.at[part, k]
                )
            )
        return moves

    early = TOGETHER + 1
    moves = incoming(0, 0, early)
    later = incoming(1, early, share - early)
    for move in moves + later:
        move.start()

    s = sketch_ref[...]
    high = s.astype(BF16).astype(F32)
    sk_ref[...] = jnp.concatenate([high, s - high], 0).astype(BF16)
    for t in range(TOGETHER):
        sys_ref[t] = jnp.concatenate([identity(rank)] * 2, 1)
    zprev[...] = jnp.zeros_like(zprev)
    geo[share] = jnp.zeros(geo.shape[1:], F32)
    for move in small + moves:
        move.wait()
    put_features(geo[0, 0], geo[0, 1], fd, fw, ru, rw)

    def outgoing(which, first, count):
        buf, out, shift = ((ybuf, left_ref, 0), (rbuf, right_ref, TOGETHER))[which]
        blocks = pl.ds(first + shift, count)
        places = pl.ds(me * share + first, count)
        here = pltpu.make_async_copy(
            buf.at[blocks, :, mine], out.at[places], out_local.at[which]
        )
        there = pltpu.make_async_remote_copy(
            src_ref=buf.at[blocks, :, theirs],
            dst_ref=out.at[places],
            send_sem=out_send.at[which],
            recv_sem=out_recv.at[which],
            device_id={"rows": other},
            device_id_type=MESH,
        )
        return here, there

    def step(m, carry):
        k = TOGETHER * m
        places = [me * share + k + t for t in range(TOGETHER)]
        deltas = [rs_ref[p] - cs_ref[p] for p in places]
        lives = [jnp.where(p < count_ref[0], 1.0, 0.0) for p in places]
        blocks_step(
            geo, k, deltas, lives, sk_ref, ybuf, rbuf, zprev, sys_ref, fd, fw, ru, rw, bh, bl
        )
        for move in outgoing(0, k, TOGETHER):
            move.start()

        @pl.when(m == 0)
        def _():
            for move in later:
                move.wait()

        @pl.when(m > 0)
        def _():
            for move in outgoing(1, k - TOGETHER, TOGETHER):
                move.start()

        return carry

    lax.fori_loop(0, share // TOGETHER, step, 0)
    systems = [eliminated(sys_ref[t], 0, rank) for t in range(TOGETHER)]
    for t in range(TOGETHER):
        rbuf[share + t] = times(systems[t][:, :rank], zprev[t])
    for move in outgoing(1, share - TOGETHER, TOGETHER):
        move.start()
    for which in range(2):
        for move in outgoing(which, 0, share):
            move.wait()


def on_device(row_geom, col_geom, row_start, col_start, block_count, sketch):
    owned, geo_count, half = row_geom.shape
    rank = sketch.shape[1]
    share, width = owned // 2, 2 * half
    hbm = pl.BlockSpec(memory_space=pl.ANY)
    dma = pltpu.SemaphoreType.DMA
    return pl.pallas_call(
        kernel,
        out_shape=[jax.ShapeDtypeStruct((owned, rank, half), F32)] * 2,
        in_specs=[hbm] * 5 + [pl.BlockSpec(memory_space=pltpu.VMEM)],
        out_specs=[hbm, hbm],
        scratch_shapes=[
            pltpu.VMEM((share + 1, 2, geo_count, width), F32),
            pltpu.VMEM((2 * rank, width), BF16),
            pltpu.VMEM((share, rank, width), F32),
            pltpu.VMEM((share + TOGETHER, rank, width), F32),
            pltpu.VMEM((TOGETHER, rank, width), F32),
            pltpu.VMEM((TOGETHER, rank, 2 * rank), F32),
            pltpu.VMEM((width, 48), BF16),
            pltpu.VMEM((width, 240), BF16),
            pltpu.VMEM((48, width), BF16),
            pltpu.VMEM((240, width), BF16),
            pltpu.VMEM((2, width, STRIPE), BF16),
            pltpu.VMEM((2, width, STRIPE), BF16),
            pltpu.SMEM(row_start.shape, jnp.int32),
            pltpu.SMEM(col_start.shape, jnp.int32),
            pltpu.SMEM(block_count.shape, jnp.int32),
            dma((3,)), dma((2, 2)), dma((2, 2)), dma((2, 2)), dma((2,)), dma((2,)), dma((2,)),
        ],
        compiler_params=pltpu.CompilerParams(
            collective_id=0, has_side_effects=True, vmem_limit_bytes=62 << 20
        ),
    )(row_start, col_start, block_count, row_geom, col_geom, sketch.T)


def solution(mesh):
    placed = (
        P("cols", None, "rows"),
        P("cols", None, "rows"),
        P("cols"),
        P("cols"),
        P("cols"),
        P(),
    )
    return jax.shard_map(
        on_device,
        mesh=mesh,
        in_specs=placed,
        out_specs=(P("cols", None, "rows"), P("cols", None, "rows")),
        check_vma=False,
    )
```
